32 devices in a mesh: dp: 16 (over z, x, core), tensor: 2 (over y).
Axes of the slice: x: 2, y: 2, z: 4, core: 2. Of those that a mesh axis runs over, the one named last changes fastest.
Arguments:
- tokens: bfloat16 [1024, 8192], P('dp'), may hold values from -6 to 6
- span_lengths: int32 [24], replicated, may hold values from 1 to 512, 1024 in all
- resume: int32 [24], replicated, may hold values 0 or 1
- slot_ids: int32 [24], replicated, may hold values from 0 to 23, each once
- in_weight: bfloat16 [2, 8192, 16384], P(None, 'dp', 'tensor'), may hold values from -0.0625 to 0.0625
- conv_weight: float32 [4, 16384], P(None, 'tensor'), may hold values from -3 to 3
- conv_bias: float32 [16384], P('tensor'), may hold values from -3 to 3
- rank_weight: bfloat16 [16384, 512], P('tensor'), may hold values from -0.046875 to 0.046875
- state_weight: bfloat16 [16384, 32], P('tensor'), may hold values from -0.09375 to 0.09375
- step_weight: bfloat16 [512, 16384], P('dp', 'tensor'), may hold values from -0.25 to 0.25
- step_bias: float32 [16384], P('tensor'), may hold values from -4 to -1
- decay_rate: float32 [16, 16384], P(None, 'tensor'), may hold values from 0.005 to 8
- skip_gain: float32 [16384], P('tensor'), may hold values from 0 to 3
- conv_cache: bfloat16 [24, 3, 16384], P(None, None, 'tensor'), may hold values from -6 to 6
- state_cache: float32 [24, 16, 16384], P(None, None, 'tensor'), may hold values from -6 to 6
- out_weight: bfloat16 [16384, 8192], P('tensor', 'dp'), may hold values from -0.046875 to 0.046875
Outputs:
- mixer_out: bfloat16 [1024, 8192], P('tensor', 'dp')
The draws below stay inside these ranges and needn't reach their ends.
Inputs may be any that keep to these rules, and one draw needn't show every extreme that they name: `span_lengths`: the 24 lengths sum to 1024; the largest is exactly 512. `slot_ids`: each slot 0 to 23 is named once.
All inputs are finite; a program needn't handle non-finite values.
Results may differ from the reference program's by a relative error of at most 0.035.
Values may be sent and summed in bfloat16 or wider, within the bound.
A program may use at most 256 MiB of HBM per device.

```python
import math
import jax
import jax.numpy as jnp
import numpy as np
from jax import lax

D = 8192
E = 16384
NS = 16
CONV = 4
R_DT = 512
SPANS = 24
ROWS = 1024
MOST = 512
N_DP = 16


def touch_ends(array, rng, low, top_value):
    shape = array.shape
    index_at = [jax.random.randint(jax.random.fold_in(rng, axis), (), 0, shape[axis]) for axis in range(len(shape))]
    array = array.at[tuple(index_at)].set(low)
    longest = shape.index(max(shape))
    index_at[longest] = (index_at[longest] + 1) % shape[longest]
    return array.at[tuple(index_at)].set(top_value)


def block_scale(stream_key, dims, pieces, low, top_value):
    gain, own = 1.0, jax.random.fold_in(stream_key, 6)
    for dim, parts in pieces:
        draws = jnp.exp(jax.random.uniform(jax.random.fold_in(own, dim), (parts,), jnp.float32, low / len(pieces), top_value / len(pieces)))
        gain = gain * jnp.repeat(draws, dims[dim] // parts).reshape([-1 if axis == dim else 1 for axis in range(len(dims))])
    return gain


def split_up(amount, total, most, lean):
    weights = [(1 << 20) // math.isqrt(standing ** lean) + 1 for standing in range(2, amount + 1)]
    surplus, holding = total - most - (amount - 1), [1] * (amount - 1)
    while surplus > 0:
        free = [i for i in range(amount - 1) if holding[i] < most]
        pool, left = sum([weights[i] for i in free]), surplus
        for i in free:
            extra = min(most - holding[i], max(1, left * weights[i] // pool), surplus)
            holding[i] = holding[i] + extra
            surplus = surplus - extra
    return np.array([most] + holding)


def uneven_parts(own_key, count, total, reach, lean):
    if count == 2:
        one = jax.random.randint(own_key, (), max(1, total - reach), min(reach, total - 1) + 1)
        return jnp.stack([one, total - one])
    lengths = jnp.asarray(split_up(count, total, reach, lean), jnp.int32)
    twos = (count - 1) // 2
    giver, receiver = lengths[1:1 + 2 * twos:2], lengths[2:2 + 2 * twos:2]
    margin = jnp.minimum(giver - 1, reach - receiver)
    moved = jax.random.randint(jax.random.fold_in(own_key, 1), (twos,), 0, 1 << 20) % (margin + 1)
    lengths = lengths.at[1:1 + 2 * twos:2].set(giver - moved).at[2:2 + 2 * twos:2].set(receiver + moved)
    return lengths[jax.random.permutation(jax.random.fold_in(own_key, 2), count)]


def normal_values(key, extent, scale, most, shards=(), held_as=jnp.bfloat16):
    result = jax.random.normal(key, extent, jnp.float32) * scale
    if len(shards) > 0:
        result = block_scale(key, extent, shards, -0.22, 0.18) * result
    return jnp.clip(result, min=-most, max=most).astype(held_as)


def setup_inputs(seed: int = 0) -> dict:
    arg_keys = jax.random.split(jax.random.key(seed), 17)
    return {
        "tokens": normal_values(arg_keys[0], (ROWS, D), 1.0, 6.0, ((0, 16),)),
        "span_lengths": uneven_parts(arg_keys[1], SPANS, ROWS, MOST, 2).astype(jnp.int32),
        "resume": touch_ends((jax.random.randint(arg_keys[2], (SPANS,), 0, 2) < 1).astype(jnp.int32), jax.random.fold_in(arg_keys[2], 1), 0, 1),
        "slot_ids": jax.random.permutation(arg_keys[3], SPANS).astype(jnp.int32),
        "in_weight": normal_values(arg_keys[4], (2, D, E), D ** -0.5, 0.0625, ((1, 16), (2, 2))),
        "conv_weight": normal_values(arg_keys[5], (CONV, E), CONV ** -0.5, 3.0, ((1, 2),), jnp.float32),
        "conv_bias": normal_values(arg_keys[6], (E,), 0.5, 3.0, ((0, 2),), jnp.float32),
        "rank_weight": normal_values(arg_keys[7], (E, R_DT), E ** -0.5, 0.046875, ((0, 2),)),
        "state_weight": normal_values(arg_keys[8], (E, 2 * NS), (E // 4) ** -0.5, 0.09375, ((0, 2),)),
        "step_weight": normal_values(arg_keys[9], (R_DT, E), R_DT ** -0.5, 0.25, ((0, 16), (1, 2))),
        "step_bias": jnp.clip(-4.0 + 3.0 * jax.random.uniform(arg_keys[10], (E,), jnp.float32) ** block_scale(arg_keys[10], (E,), ((0, 2),), -0.2, 0.2), -4.0, -1.0),
        "decay_rate": jnp.clip(jnp.exp(math.log(8.0) - 7.377759 * jax.random.uniform(arg_keys[11], (NS, E), jnp.float32) ** block_scale(arg_keys[11], (NS, E), ((1, 2),), -0.2, 0.2)), 0.005, 8.0),
        "skip_gain": jnp.clip(3.0 * jax.random.uniform(arg_keys[12], (E,), jnp.float32) ** block_scale(arg_keys[12], (E,), ((0, 2),), -0.2, 0.2), 0.0, 3.0),
        "conv_cache": normal_values(arg_keys[13], (SPANS, CONV - 1, E), 1.0, 6.0, ((2, 2),)),
        "state_cache": normal_values(arg_keys[14], (SPANS, NS, E), 1.0, 6.0, ((2, 2),), jnp.float32),
        "out_weight": normal_values(arg_keys[15], (E, D), E ** -0.5, 0.046875, ((0, 2), (1, 16))),
    }


def reference(tokens, span_lengths, resume, slot_ids, in_weight, conv_weight, conv_bias, rank_weight, state_weight, step_weight, step_bias, decay_rate, skip_gain, conv_cache, state_cache, out_weight):
    row_count = tokens.shape[0]
    blocks = D // N_DP

    def add_block(running, block_index):
        offset = (block_index * blocks).astype(jnp.int32)
        token_part = lax.dynamic_slice_in_dim(tokens, offset, blocks, 1)
        weight_part = lax.dynamic_slice_in_dim(in_weight, offset, blocks, 1)
        term_inner = jnp.dot(token_part, weight_part[0], preferred_element_type=jnp.float32).astype(jnp.bfloat16)
        term_gate = jnp.dot(token_part, weight_part[1], preferred_element_type=jnp.float32).astype(jnp.bfloat16)
        term_inner, term_gate = lax.optimization_barrier((term_inner, term_gate))
        return ((running[0] + term_inner.astype(jnp.float32), running[1] + term_gate.astype(jnp.float32)), None)
    zero_sums = jnp.zeros((row_count, E), jnp.float32)
    (sum_inner, sum_gate), _ = lax.scan(add_block, (zero_sums, zero_sums), jnp.arange(N_DP, dtype=jnp.int32))
    inner_rows = sum_inner.astype(jnp.bfloat16)
    gate_rows = sum_gate.astype(jnp.bfloat16)
    span_ends = jnp.cumsum(span_lengths).astype(jnp.int32)
    span_starts = span_ends - span_lengths
    row_ids = jnp.arange(row_count, dtype=jnp.int32)
    owners = lax.optimization_barrier(jnp.sum((span_ends[None, :] <= row_ids[:, None]).astype(jnp.int32), axis=1))
    one_hot = (owners[:, None] == jnp.arange(SPANS, dtype=jnp.int32)[None, :]).astype(jnp.int32)
    position = row_ids - lax.optimization_barrier(jnp.sum(one_hot * span_starts[None, :], axis=1))
    row_slot = lax.optimization_barrier(jnp.sum(one_hot * slot_ids[None, :], axis=1)).astype(jnp.int32)
    row_resume = lax.optimization_barrier(jnp.sum(one_hot * resume[None, :], axis=1)).astype(jnp.int32)
    inner_wide = inner_rows.astype(jnp.float32)
    cached = conv_cache[row_slot].astype(jnp.float32)
    convolved = conv_bias[None, :] + conv_weight[0][None, :] * inner_wide
    for lagged in range(1, CONV):
        earlier = jnp.concatenate([jnp.zeros((lagged, E), jnp.float32), inner_wide[:row_count - lagged]], axis=0)
        cache_index = CONV - 1 + position - lagged
        pick = (jnp.arange(CONV - 1, dtype=jnp.int32)[None, :] == cache_index[:, None])[:, :, None]
        from_cache = lax.optimization_barrier(jnp.sum(jnp.where(pick, cached, 0.0), axis=1)) * row_resume[:, None].astype(jnp.float32)
        convolved = convolved + conv_weight[lagged][None, :] * jnp.where((position >= lagged)[:, None], earlier, from_cache)
    activated = jax.nn.silu(convolved).astype(jnp.bfloat16)
    rank_sum = jnp.dot(activated, rank_weight, preferred_element_type=jnp.float32)
    state_sum = jnp.dot(activated, state_weight, preferred_element_type=jnp.float32)
    rank_normed = (rank_sum * lax.rsqrt(lax.optimization_barrier(jnp.mean(rank_sum * rank_sum, axis=1, keepdims=True)) + 1e-06)).astype(jnp.bfloat16)
    step_size = jax.nn.softplus(jnp.dot(rank_normed, step_weight, preferred_element_type=jnp.float32) + step_bias[None, :])
    input_map = state_sum[:, :NS]
    output_map = state_sum[:, NS:]
    active_float = activated.astype(jnp.float32)

    def advance(state, inputs):
        value_row, step_row, input_row, output_row, slot_row, flag_row, place_row = inputs
        restored = state_cache[slot_row] * flag_row.astype(jnp.float32)
        prior = jnp.where(place_row == 0, restored, state)
        state = jnp.exp(-step_row[None, :] * decay_rate) * prior + (step_row * value_row)[None, :] * input_row[:, None]
        return (state, lax.optimization_barrier(jnp.sum(output_row[:, None] * state, axis=0)))
    _, scanned = lax.scan(advance, jnp.zeros((NS, E), jnp.float32), (active_float, step_size, input_map, output_map, row_slot, row_resume, position))
    scan_out = scanned + skip_gain[None, :] * active_float
    gated = (scan_out * jax.nn.silu(gate_rows.astype(jnp.float32))).astype(jnp.bfloat16)
    return jnp.dot(gated, out_weight, preferred_element_type=jnp.float32).astype(jnp.bfloat16)
```

```python
import jax
import jax.numpy as jnp
import numpy as np
from jax import lax
from jax.experimental import pallas as pl
from jax.experimental.pallas import tpu as pltpu
from jax.sharding import PartitionSpec as P

NS = 16
CONV = 4
F32 = jnp.float32
BF16 = jnp.bfloat16


def rings(devices):
    chips = devices // 2
    order = list(range(0, chips, 2)) + list(range(0, chips, 2))[::-1]
    order = [c if i < (chips + 1) // 2 else c + 1 for i, c in enumerate(order)][:chips]
    table = np.array([order, [order[-p % chips] for p in range(chips)]], np.int32)
    place = np.zeros((2, chips), np.int32)
    for core in range(2):
        place[core, table[core]] = np.arange(chips)
    along = [
        (2 * int(table[core, p]) + core, 2 * int(table[core, (p + 1) % chips]) + core)
        for core in range(2)
        for p in range(chips)
    ]
    across = [(i, i ^ 1) for i in range(devices)]
    return chips, table, place, along, across


def normalize(rank_sum):
    return (
        rank_sum * lax.rsqrt(jnp.mean(rank_sum * rank_sum, axis=1, keepdims=True) + 1e-06)
    ).astype(BF16)


def scan_kernel(
    owner_ref, open_ref, step_ref, act_ref, gate_ref, in_ref, out_map_ref, decay_ref, restored_ref,
    skip_ref, init_ref, gated_ref, last_ref, state_ref, drive_ref, sums_ref,
):
    block = pl.program_id(0)
    rows, width = step_ref.shape
    copies = width // in_ref.shape[2]

    @pl.when(block == 0)
    def _():
        state_ref[...] = init_ref[...]

    drive_ref[...] = step_ref[...] * act_ref[...].astype(F32)
    decay = decay_ref[...]

    def wide(a):
        return a if copies == 1 else jnp.concatenate([a] * copies, axis=1)

    def group(g, state):
        for r in range(8):
            t = g * 8 + r
            row = block * rows + t
            opening = jnp.full(state.shape, open_ref[row], jnp.int32) > 0
            prior = jnp.where(opening, restored_ref[owner_ref[row]], state)
            fading = jnp.exp2(step_ref[pl.ds(t, 1), :] * decay)
            state = fading * prior + drive_ref[pl.ds(t, 1), :] * wide(in_ref[t])
            sums_ref[pl.ds(t, 1), :] = jnp.sum(wide(out_map_ref[t]) * state, axis=0, keepdims=True)
        return state

    state = lax.fori_loop(0, rows // 8, group, state_ref[...])
    state_ref[...] = state
    last_ref[...] = state
    gate = gate_ref[...].astype(F32)
    scan_out = sums_ref[...] + skip_ref[...] * act_ref[...].astype(F32)
    gated_ref[...] = (scan_out * (gate / (1.0 + jnp.exp(-gate)))).astype(BF16)


def scan_rows(owners, opens, step, act, gate, in_map, out_map, decay, restored, skip, init):
    total, width = step.shape
    rows = 128
    lanes = in_map.shape[2]
    by_row = pl.BlockSpec((rows, width), lambda i, *_: (i, 0))
    maps = pl.BlockSpec((rows, NS, lanes), lambda i, *_: (i, 0, 0))

    def whole(a):
        return pl.BlockSpec(a.shape, lambda i, *_: (0,) * a.ndim)

    return pl.pallas_call(
        scan_kernel,
        out_shape=(
            jax.ShapeDtypeStruct((total, width), BF16),
            jax.ShapeDtypeStruct((NS, width), F32),
        ),
        grid_spec=pltpu.PrefetchScalarGridSpec(
            num_scalar_prefetch=2,
            grid=(total // rows,),
            in_specs=[by_row, by_row, by_row, maps, maps]
            + [whole(a) for a in (decay, restored, skip, init)],
            out_specs=(by_row, whole(init)),
            scratch_shapes=[
                pltpu.VMEM((NS, width), F32),
                pltpu.VMEM((rows, width), F32),
                pltpu.VMEM((rows, width), F32),
            ],
        ),
        compiler_params=pltpu.CompilerParams(vmem_limit_bytes=32 * 1024 * 1024),
        cost_estimate=pl.CostEstimate(
            flops=total * NS * width * 8,
            bytes_accessed=total * (2 * NS * lanes * 4 + width * 10),
            transcendentals=total * NS * width,
        ),
    )(owners, opens, step, act, gate, in_map, out_map, decay, restored, skip, init)


def shards(
    tokens,
    span_lengths,
    resume,
    slot_ids,
    in_weight,
    conv_weight,
    conv_bias,
    rank_weight,
    state_weight,
    step_weight,
    step_bias,
    decay_rate,
    skip_gain,
    conv_cache,
    state_cache,
    out_weight,
):
    devices = lax.axis_size("dp")
    tensor = lax.axis_size("tensor")
    rows = tokens.shape[0] * devices
    width = in_weight.shape[2] // devices
    ranks = rank_weight.shape[1]
    spans = span_lengths.shape[0]
    me = lax.axis_index("dp")
    core, chip = me % 2, me // 2
    chips, table, place, along, across = rings(devices)
    table, place = jnp.asarray(table), jnp.asarray(place)

    def channels(a, owner, axis):
        return lax.dynamic_slice_in_dim(a, owner * width, width, axis)

    def block_at(which, step):
        return 2 * table[which, (place[which, chip] - step) % chips] + which

    columns = lax.all_to_all(tokens, "dp", split_axis=1, concat_axis=0, tiled=True)

    halves = []
    for half in range(2):
        arrived = None
        for step in range(chips):
            mine, other = block_at(core, step + 1), block_at(1 - core, step + 1)
            theirs = jnp.dot(
                columns, channels(in_weight[half], other, 1), preferred_element_type=F32
            ).astype(BF16)
            own = jnp.dot(
                columns, channels(in_weight[half], mine, 1), preferred_element_type=F32
            ).astype(BF16)
            total = own.astype(F32) + lax.ppermute(theirs, "dp", across).astype(F32)
            if step > 0:
                total = total + arrived.astype(F32)
            total = total.astype(BF16)
            if step < chips - 1:
                arrived = lax.ppermute(total, "dp", along)
        halves.append(total)
    inner_rows, gate_rows = halves

    span_ends = jnp.cumsum(span_lengths)
    span_starts = span_ends - span_lengths
    row_ids = jnp.arange(rows, dtype=jnp.int32)
    owners = jnp.sum((span_ends[None, :] <= row_ids[:, None]).astype(jnp.int32), axis=1)
    one_hot = (owners[:, None] == jnp.arange(spans, dtype=jnp.int32)[None, :]).astype(jnp.int32)
    position = row_ids - jnp.sum(one_hot * span_starts[None, :], axis=1)
    row_resume = jnp.sum(one_hot * resume[None, :], axis=1)

    span_cache = channels(conv_cache, me, 2)[slot_ids].reshape(spans * (CONV - 1), width)
    inner_wide = inner_rows.astype(F32)
    taps = channels(conv_weight, me, 1)
    convolved = channels(conv_bias, me, 0)[None, :] + taps[0][None, :] * inner_wide
    for lagged in range(1, CONV):
        earlier = jnp.concatenate(
            [jnp.zeros((lagged, width), F32), inner_wide[: rows - lagged]], axis=0
        )
        wanted = jnp.where(
            (position < lagged) & (row_resume > 0),
            owners * (CONV - 1) + CONV - 1 + position - lagged,
            -1,
        )
        pick = (
            wanted[:, None] == jnp.arange(spans * (CONV - 1), dtype=jnp.int32)[None, :]
        ).astype(BF16)
        from_cache = jnp.dot(pick, span_cache, preferred_element_type=F32)
        convolved = convolved + taps[lagged][None, :] * jnp.where(
            (position >= lagged)[:, None], earlier, from_cache
        )
    activated = jax.nn.silu(convolved).astype(BF16)

    both = jnp.concatenate([channels(rank_weight, me, 0), channels(state_weight, me, 0)], axis=1)
    parts = jnp.dot(activated, both, preferred_element_type=F32).astype(BF16)
    parts = lax.all_to_all(
        parts.reshape(devices, rows // devices, -1), "dp", split_axis=0, concat_axis=0, tiled=True
    )
    sums = lax.psum(jnp.sum(parts.astype(F32), axis=0).astype(BF16), "tensor").astype(F32)
    ready = jnp.concatenate([normalize(sums[:, :ranks]), sums[:, ranks:].astype(BF16)], axis=1)
    ready = lax.all_gather(ready, "dp", axis=0, tiled=True)
    rank_normed, state_sum = ready[:, :ranks], ready[:, ranks:].astype(F32)

    step_local = lax.all_to_all(step_weight, "dp", split_axis=1, concat_axis=0, tiled=True)
    step_size = jax.nn.softplus(
        jnp.dot(rank_normed, step_local, preferred_element_type=F32)
        + channels(step_bias, me, 0)[None, :]
    )
    lanes = min(128, width)
    in_map = jnp.broadcast_to(state_sum[:, :NS, None], (rows, NS, lanes))
    out_map = jnp.broadcast_to(state_sum[:, NS:, None], (rows, NS, lanes))
    decay = channels(decay_rate, me, 1) * (-1.0 / np.log(2.0)).astype(np.float32)
    restored = channels(state_cache, me, 2)[slot_ids] * resume[:, None, None].astype(F32)
    skip = channels(skip_gain, me, 0)[None, :]
    opens = (position == 0).astype(jnp.int32)

    state = jnp.zeros((NS, width), F32)
    part_rows = rows // 2
    partials = []
    for part in range(2):
        cut = slice(part * part_rows, (part + 1) * part_rows)
        held, state = scan_rows(
            owners[cut], opens[cut], step_size[cut], activated[cut], gate_rows[cut], in_map[cut],
            out_map[cut], decay, restored, skip, state,
        )
        total = jnp.zeros((part_rows, out_weight.shape[1]), F32)
        for step in range(chips):
            mine, other = block_at(core, step), block_at(1 - core, step)
            theirs = lax.ppermute(held, "dp", across)
            total = total + jnp.dot(
                held, channels(out_weight, mine, 0), preferred_element_type=F32
            )
            total = total + jnp.dot(
                theirs, channels(out_weight, other, 0), preferred_element_type=F32
            )
            if step < chips - 1:
                held = lax.ppermute(held, "dp", along)
        partials.append(total.astype(BF16))
    if tensor == 2:
        first = lax.axis_index("tensor") == 0
        send = jnp.where(first, partials[1], partials[0])
        keep = jnp.where(first, partials[0], partials[1])
        got = lax.ppermute(send, "tensor", [(0, 1), (1, 0)])
        return (keep.astype(F32) + got.astype(F32)).astype(BF16)
    return lax.psum_scatter(
        jnp.concatenate(partials, axis=0), "tensor", scatter_dimension=0, tiled=True
    )


def solution(mesh):
    return jax.shard_map(
        shards,
        mesh=mesh,
        in_specs=(
            P("dp", None),
            P(),
            P(),
            P(),
            P(None, "dp", "tensor"),
            P(None, "tensor"),
            P("tensor"),
            P("tensor", None),
            P("tensor", None),
            P("dp", "tensor"),
            P("tensor"),
            P(None, "tensor"),
            P("tensor"),
            P(None, None, "tensor"),
            P(None, None, "tensor"),
            P("tensor", "dp"),
        ),
        out_specs=P("tensor", "dp"),
        check_vma=False,
    )
```

```python
import jax
import jax.numpy as jnp
import numpy as np
from jax import lax
from jax.experimental import pallas as pl
from jax.experimental.pallas import tpu as pltpu
from jax.sharding import PartitionSpec as P

NS = 16
CONV = 4
F32 = jnp.float32
BF16 = jnp.bfloat16


def rings(devices):
    chips = devices // 2
    order = list(range(0, chips, 2)) + list(range(0, chips, 2))[::-1]
    order = [c if i < (chips + 1) // 2 else c + 1 for i, c in enumerate(order)][:chips]
    table = np.array([order, [order[-p % chips] for p in range(chips)]], np.int32)
    place = np.zeros((2, chips), np.int32)
    for core in range(2):
        place[core, table[core]] = np.arange(chips)
    along = [
        (2 * int(table[core, p]) + core, 2 * int(table[core, (p + 1) % chips]) + core)
        for core in range(2)
        for p in range(chips)
    ]
    across = [(i, i ^ 1) for i in range(devices)]
    return chips, table, place, along, across


def normalize(rank_sum):
    return (
        rank_sum * lax.rsqrt(jnp.mean(rank_sum * rank_sum, axis=1, keepdims=True) + 1e-06)
    ).astype(BF16)


def scan_kernel(
    slot_ref, open_ref, step_ref, act_ref, gate_ref, in_ref, out_map_ref, decay_ref, restored_ref,
    skip_ref, init_ref, gated_ref, last_ref, state_ref, drive_ref, sums_ref,
):
    block = pl.program_id(0)
    rows, width = step_ref.shape
    copies = width // in_ref.shape[2]

    @pl.when(block == 0)
    def _():
        state_ref[...] = init_ref[...]

    drive_ref[...] = step_ref[...] * act_ref[...].astype(F32)
    decay = decay_ref[...]

    def wide(a):
        return a if copies == 1 else jnp.concatenate([a] * copies, axis=1)

    def group(g, state):
        for r in range(8):
            t = g * 8 + r
            row = block * rows + t
            opening = jnp.full(state.shape, open_ref[row], jnp.int32) > 0
            prior = jnp.where(opening, restored_ref[slot_ref[row]], state)
            fading = jnp.exp2(step_ref[pl.ds(t, 1), :] * decay)
            state = fading * prior + drive_ref[pl.ds(t, 1), :] * wide(in_ref[t])
            sums_ref[pl.ds(t, 1), :] = jnp.sum(wide(out_map_ref[t]) * state, axis=0, keepdims=True)
        return state

    state = lax.fori_loop(0, rows // 8, group, state_ref[...])
    state_ref[...] = state
    last_ref[...] = state
    gate = gate_ref[...].astype(F32)
    scan_out = sums_ref[...] + skip_ref[...] * act_ref[...].astype(F32)
    gated_ref[...] = (scan_out * (gate / (1.0 + jnp.exp(-gate)))).astype(BF16)


def scan_rows(slots, opens, step, act, gate, in_map, out_map, decay, restored, skip, init):
    total, width = step.shape
    rows = 128
    lanes = in_map.shape[2]
    by_row = pl.BlockSpec((rows, width), lambda i, *_: (i, 0))
    maps = pl.BlockSpec((rows, NS, lanes), lambda i, *_: (i, 0, 0))

    def whole(a):
        return pl.BlockSpec(a.shape, lambda i, *_: (0,) * a.ndim)

    return pl.pallas_call(
        scan_kernel,
        out_shape=(
            jax.ShapeDtypeStruct((total, width), BF16),
            jax.ShapeDtypeStruct((NS, width), F32),
        ),
        grid_spec=pltpu.PrefetchScalarGridSpec(
            num_scalar_prefetch=2,
            grid=(total // rows,),
            in_specs=[by_row, by_row, by_row, maps, maps]
            + [whole(a) for a in (decay, restored, skip, init)],
            out_specs=(by_row, whole(init)),
            scratch_shapes=[
                pltpu.VMEM((NS, width), F32),
                pltpu.VMEM((rows, width), F32),
                pltpu.VMEM((rows, width), F32),
            ],
        ),
        compiler_params=pltpu.CompilerParams(vmem_limit_bytes=32 * 1024 * 1024),
        cost_estimate=pl.CostEstimate(
            flops=total * NS * width * 2400,
            bytes_accessed=total * (2 * NS * lanes * 4 + width * 10),
            transcendentals=total * NS * width,
        ),
    )(slots, opens, step, act, gate, in_map, out_map, decay, restored, skip, init)


def shards(
    tokens,
    span_lengths,
    resume,
    slot_ids,
    in_weight,
    conv_weight,
    conv_bias,
    rank_weight,
    state_weight,
    step_weight,
    step_bias,
    decay_rate,
    skip_gain,
    conv_cache,
    state_cache,
    out_weight,
):
    devices = lax.axis_size("dp")
    tensor = lax.axis_size("tensor")
    rows = tokens.shape[0] * devices
    width = in_weight.shape[2] // devices
    ranks = rank_weight.shape[1]
    spans = span_lengths.shape[0]
    me = lax.axis_index("dp")
    core, chip = me % 2, me // 2
    chips, table, place, along, across = rings(devices)
    table, place = jnp.asarray(table), jnp.asarray(place)

    def channels(a, owner, axis):
        return lax.dynamic_slice_in_dim(a, owner * width, width, axis)

    def block_at(which, step):
        return 2 * table[which, (place[which, chip] - step) % chips] + which

    columns = lax.all_to_all(tokens, "dp", split_axis=1, concat_axis=0, tiled=True)

    step_local = lax.all_to_all(step_weight, "dp", split_axis=1, concat_axis=0, tiled=True)
    part_rows = rows // 2
    cuts = [slice(part * part_rows, (part + 1) * part_rows) for part in range(2)]

    halves = []
    for half in range(2):
        arrived = [None, None]
        for step in range(chips):
            mine, other = block_at(core, step + 1), block_at(1 - core, step + 1)
            theirs = jnp.dot(
                columns, channels(in_weight[half], other, 1), preferred_element_type=F32
            ).astype(BF16)
            theirs = lax.ppermute(theirs, "dp", across)
            weight = channels(in_weight[half], mine, 1)
            totals = []
            for part, cut in enumerate(cuts):
                own = jnp.dot(columns[cut], weight, preferred_element_type=F32).astype(BF16)
                total = own.astype(F32) + theirs[cut].astype(F32)
                if step > 0:
                    total = total + arrived[part].astype(F32)
                total = total.astype(BF16)
                if half == 1 and step == 0:
                    total, _ = lax.optimization_barrier((total, inner_arrived[part]))
                totals.append(total)
            if step < chips - 1:
                arrived = [lax.ppermute(total, "dp", along) for total in totals]
                if half == 0 and step == chips // 2:
                    arrived[0], step_local = lax.optimization_barrier((arrived[0], step_local))
            if half == 0 and step == chips - 2:
                inner_arrived = arrived
        halves.append(jnp.concatenate(totals, axis=0))
    inner_rows, gate_rows = halves

    span_ends = jnp.cumsum(span_lengths)
    span_starts = span_ends - span_lengths
    row_ids = jnp.arange(rows, dtype=jnp.int32)
    owners = jnp.sum((span_ends[None, :] <= row_ids[:, None]).astype(jnp.int32), axis=1)
    one_hot = (owners[:, None] == jnp.arange(spans, dtype=jnp.int32)[None, :]).astype(jnp.int32)
    position = row_ids - jnp.sum(one_hot * span_starts[None, :], axis=1)
    row_slot = jnp.sum(one_hot * slot_ids[None, :], axis=1)
    row_resume = jnp.sum(one_hot * resume[None, :], axis=1)
    slots = jnp.arange(spans, dtype=jnp.int32)
    slot_resume = jnp.sum((slot_ids[:, None] == slots[None, :]) * resume[:, None], axis=0)

    slot_cache = channels(conv_cache, me, 2).reshape(spans * (CONV - 1), width)
    inner_wide = inner_rows.astype(F32)
    taps = channels(conv_weight, me, 1)
    convolved = channels(conv_bias, me, 0)[None, :] + taps[0][None, :] * inner_wide
    for lagged in range(1, CONV):
        earlier = jnp.concatenate(
            [jnp.zeros((lagged, width), F32), inner_wide[: rows - lagged]], axis=0
        )
        wanted = jnp.where(
            (position < lagged) & (row_resume > 0),
            row_slot * (CONV - 1) + CONV - 1 + position - lagged,
            -1,
        )
        pick = (
            wanted[:, None] == jnp.arange(spans * (CONV - 1), dtype=jnp.int32)[None, :]
        ).astype(BF16)
        from_cache = jnp.dot(pick, slot_cache, preferred_element_type=F32)
        convolved = convolved + taps[lagged][None, :] * jnp.where(
            (position >= lagged)[:, None], earlier, from_cache
        )
    activated = jax.nn.silu(convolved).astype(BF16)

    both = jnp.concatenate([channels(rank_weight, me, 0), channels(state_weight, me, 0)], axis=1)
    parts = jnp.dot(activated, both, preferred_element_type=F32).astype(BF16)
    parts = lax.all_to_all(
        parts.reshape(devices, rows // devices, -1), "dp", split_axis=0, concat_axis=0, tiled=True
    )
    sums = jnp.sum(parts.astype(F32), axis=0).astype(BF16)
    if tensor == 2:
        sums = sums.astype(F32) + lax.ppermute(sums, "tensor", [(0, 1), (1, 0)]).astype(F32)
    else:
        sums = lax.psum(sums, "tensor").astype(F32)
    ready = jnp.concatenate([normalize(sums[:, :ranks]), sums[:, ranks:].astype(BF16)], axis=1)
    ready = lax.all_gather(ready, "dp", axis=0, tiled=True)
    rank_normed, state_sum = ready[:, :ranks], ready[:, ranks:].astype(F32)

    step_size = jax.nn.softplus(
        jnp.dot(rank_normed, step_local, preferred_element_type=F32)
        + channels(step_bias, me, 0)[None, :]
    )
    lanes = min(128, width)
    in_map = jnp.broadcast_to(state_sum[:, :NS, None], (rows, NS, lanes))
    out_map = jnp.broadcast_to(state_sum[:, NS:, None], (rows, NS, lanes))
    decay = channels(decay_rate, me, 1) * (-1.0 / np.log(2.0)).astype(np.float32)
    restored = channels(state_cache, me, 2) * slot_resume[:, None, None].astype(F32)
    skip = channels(skip_gain, me, 0)[None, :]
    opens = (position == 0).astype(jnp.int32)

    state = jnp.zeros((NS, width), F32)
    partials = []
    for part, cut in enumerate(cuts):
        held, state = scan_rows(
            row_slot[cut], opens[cut], step_size[cut], activated[cut], gate_rows[cut], in_map[cut],
            out_map[cut], decay, restored, skip, state,
        )
        total = jnp.zeros((part_rows, out_weight.shape[1]), F32)
        for step in range(chips):
            mine, other = block_at(core, step), block_at(1 - core, step)
            theirs = lax.ppermute(held, "dp", across)
            if part == 0 and step == 0:
                state, theirs = lax.optimization_barrier((state, theirs))
            total = total + jnp.dot(
                held, channels(out_weight, mine, 0), preferred_element_type=F32
            )
            total = total + jnp.dot(
                theirs, channels(out_weight, other, 0), preferred_element_type=F32
            )
            if step < chips - 1:
                held = lax.ppermute(held, "dp", along)
        partials.append(total.astype(BF16))
    if tensor == 2:
        first = lax.axis_index("tensor") == 0
        send = jnp.where(first, partials[1], partials[0])
        keep = jnp.where(first, partials[0], partials[1])
        got = lax.ppermute(send, "tensor", [(0, 1), (1, 0)])
        return (keep.astype(F32) + got.astype(F32)).astype(BF16)
    return lax.psum_scatter(
        jnp.concatenate(partials, axis=0), "tensor", scatter_dimension=0, tiled=True
    )


def solution(mesh):
    return jax.shard_map(
        shards,
        mesh=mesh,
        in_specs=(
            P("dp", None),
            P(),
            P(),
            P(),
            P(None, "dp", "tensor"),
            P(None, "tensor"),
            P("tensor"),
            P("tensor", None),
            P("tensor", None),
            P("dp", "tensor"),
            P("tensor"),
            P(None, "tensor"),
            P("tensor"),
            P(None, None, "tensor"),
            P(None, None, "tensor"),
            P("tensor", "dp"),
        ),
        out_specs=P("tensor", "dp"),
        check_vma=False,
    )
```

```python
import jax
import jax.numpy as jnp
import numpy as np
from jax import lax
from jax.experimental import pallas as pl
from jax.experimental.pallas import tpu as pltpu
from jax.sharding import PartitionSpec as P

NS = 16
CONV = 4
F32 = jnp.float32
BF16 = jnp.bfloat16


def rings(devices):
    chips = devices // 2
    order = list(range(0, chips, 2)) + list(range(0, chips, 2))[::-1]
    order = [c if i < (chips + 1) // 2 else c + 1 for i, c in enumerate(order)][:chips]
    table = np.array([order, [order[-p % chips] for p in range(chips)]], np.int32)
    place = np.zeros((2, chips), np.int32)
    for core in range(2):
        place[core, table[core]] = np.arange(chips)
    along = [
        (2 * int(table[core, p]) + core, 2 * int(table[core, (p + 1) % chips]) + core)
        for core in range(2)
        for p in range(chips)
    ]
    across = [(i, i ^ 1) for i in range(devices)]
    return chips, table, place, along, across


def normalize(rank_sum):
    return (
        rank_sum * lax.rsqrt(jnp.mean(rank_sum * rank_sum, axis=1, keepdims=True) + 1e-06)
    ).astype(BF16)


def scan_kernel(
    slot_ref, open_ref, step_ref, act_ref, gate_ref, in_ref, out_map_ref, decay_ref, restored_ref,
    skip_ref, init_ref, gated_ref, last_ref, state_ref, drive_ref, sums_ref,
):
    block = pl.program_id(0)
    rows, width = step_ref.shape
    copies = width // in_ref.shape[2]

    @pl.when(block == 0)
    def _():
        state_ref[...] = init_ref[...]

    drive_ref[...] = step_ref[...] * act_ref[...].astype(F32)
    decay = decay_ref[...]

    def wide(a):
        return a if copies == 1 else jnp.concatenate([a] * copies, axis=1)

    def group(g, state):
        for r in range(8):
            t = g * 8 + r
            row = block * rows + t
            opening = jnp.full(state.shape, open_ref[row], jnp.int32) > 0
            prior = jnp.where(opening, restored_ref[slot_ref[row]], state)
            fading = jnp.exp2(step_ref[pl.ds(t, 1), :] * decay)
            state = fading * prior + drive_ref[pl.ds(t, 1), :] * wide(in_ref[t])
            sums_ref[pl.ds(t, 1), :] = jnp.sum(wide(out_map_ref[t]) * state, axis=0, keepdims=True)
        return state

    state = lax.fori_loop(0, rows // 8, group, state_ref[...])
    state_ref[...] = state
    last_ref[...] = state
    gate = gate_ref[...].astype(F32)
    scan_out = sums_ref[...] + skip_ref[...] * act_ref[...].astype(F32)
    gated_ref[...] = (scan_out * (gate / (1.0 + jnp.exp(-gate)))).astype(BF16)


def scan_rows(slots, opens, step, act, gate, in_map, out_map, decay, restored, skip, init):
    total, width = step.shape
    rows = 128
    lanes = in_map.shape[2]
    by_row = pl.BlockSpec((rows, width), lambda i, *_: (i, 0))
    maps = pl.BlockSpec((rows, NS, lanes), lambda i, *_: (i, 0, 0))

    def whole(a):
        return pl.BlockSpec(a.shape, lambda i, *_: (0,) * a.ndim)

    return pl.pallas_call(
        scan_kernel,
        out_shape=(
            jax.ShapeDtypeStruct((total, width), BF16),
            jax.ShapeDtypeStruct((NS, width), F32),
        ),
        grid_spec=pltpu.PrefetchScalarGridSpec(
            num_scalar_prefetch=2,
            grid=(total // rows,),
            in_specs=[by_row, by_row, by_row, maps, maps]
            + [whole(a) for a in (decay, restored, skip, init)],
            out_specs=(by_row, whole(init)),
            scratch_shapes=[
                pltpu.VMEM((NS, width), F32),
                pltpu.VMEM((rows, width), F32),
                pltpu.VMEM((rows, width), F32),
            ],
        ),
        compiler_params=pltpu.CompilerParams(vmem_limit_bytes=32 * 1024 * 1024),
        cost_estimate=pl.CostEstimate(
            flops=total * NS * width * 8,
            bytes_accessed=total * (2 * NS * lanes * 4 + width * 10),
            transcendentals=total * NS * width,
        ),
    )(slots, opens, step, act, gate, in_map, out_map, decay, restored, skip, init)


def shards(
    tokens,
    span_lengths,
    resume,
    slot_ids,
    in_weight,
    conv_weight,
    conv_bias,
    rank_weight,
    state_weight,
    step_weight,
    step_bias,
    decay_rate,
    skip_gain,
    conv_cache,
    state_cache,
    out_weight,
):
    devices = lax.axis_size("dp")
    tensor = lax.axis_size("tensor")
    rows = tokens.shape[0] * devices
    width = in_weight.shape[2] // devices
    ranks = rank_weight.shape[1]
    spans = span_lengths.shape[0]
    me = lax.axis_index("dp")
    core, chip = me % 2, me // 2
    chips, table, place, along, across = rings(devices)
    table, place = jnp.asarray(table), jnp.asarray(place)

    def channels(a, owner, axis):
        return lax.dynamic_slice_in_dim(a, owner * width, width, axis)

    def entry(half, owner):
        start = (half, 0, owner * width)
        return lax.dynamic_slice(in_weight, start, (1, in_weight.shape[1], width))[0]

    def block_at(which, step):
        return 2 * table[which, (place[which, chip] - step) % chips] + which

    columns = lax.all_to_all(tokens, "dp", split_axis=1, concat_axis=0, tiled=True)

    part_rows = rows // 2
    cuts = [slice(part * part_rows, (part + 1) * part_rows) for part in range(2)]

    halves = []
    for half in range(2):
        arrived = None
        for step in range(chips):
            mine, other = block_at(core, step + 1), block_at(1 - core, step + 1)
            theirs = jnp.dot(
                columns, entry(half, other), preferred_element_type=F32
            ).astype(BF16)
            own = jnp.dot(
                columns, entry(half, mine), preferred_element_type=F32
            ).astype(BF16)
            total = own.astype(F32) + lax.ppermute(theirs, "dp", across).astype(F32)
            if step > 0:
                total = total + arrived.astype(F32)
            total = total.astype(BF16)
            if step < chips - 1:
                arrived = lax.ppermute(total, "dp", along)
                if half == 0 and step == 1:
                    arrived, step_weight = lax.optimization_barrier((arrived, step_weight))
                    step_local = lax.all_to_all(
                        step_weight, "dp", split_axis=1, concat_axis=0, tiled=True
                    )
                if half == 0 and step == chips // 2:
                    arrived, step_local = lax.optimization_barrier((arrived, step_local))
        halves.append(total)
    inner_rows, gate_rows = halves

    span_ends = jnp.cumsum(span_lengths)
    span_starts = span_ends - span_lengths
    row_ids = jnp.arange(rows, dtype=jnp.int32)
    owners = jnp.sum((span_ends[None, :] <= row_ids[:, None]).astype(jnp.int32), axis=1)
    one_hot = (owners[:, None] == jnp.arange(spans, dtype=jnp.int32)[None, :]).astype(jnp.int32)
    position = row_ids - jnp.sum(one_hot * span_starts[None, :], axis=1)
    row_slot = jnp.sum(one_hot * slot_ids[None, :], axis=1)
    row_resume = jnp.sum(one_hot * resume[None, :], axis=1)
    slots = jnp.arange(spans, dtype=jnp.int32)
    slot_resume = jnp.sum((slot_ids[:, None] == slots[None, :]) * resume[:, None], axis=0)

    slot_cache = channels(conv_cache, me, 2).reshape(spans * (CONV - 1), width)
    inner_wide = inner_rows.astype(F32)
    taps = channels(conv_weight, me, 1)
    convolved = channels(conv_bias, me, 0)[None, :] + taps[0][None, :] * inner_wide
    for lagged in range(1, CONV):
        earlier = jnp.concatenate(
            [jnp.zeros((lagged, width), F32), inner_wide[: rows - lagged]], axis=0
        )
        wanted = jnp.where(
            (position < lagged) & (row_resume > 0),
            row_slot * (CONV - 1) + CONV - 1 + position - lagged,
            -1,
        )
        pick = (
            wanted[:, None] == jnp.arange(spans * (CONV - 1), dtype=jnp.int32)[None, :]
        ).astype(BF16)
        from_cache = jnp.dot(pick, slot_cache, preferred_element_type=F32)
        convolved = convolved + taps[lagged][None, :] * jnp.where(
            (position >= lagged)[:, None], earlier, from_cache
        )
    activated = jax.nn.silu(convolved).astype(BF16)

    both = jnp.concatenate([channels(rank_weight, me, 0), channels(state_weight, me, 0)], axis=1)
    parts = jnp.dot(activated, both, preferred_element_type=F32).astype(BF16)
    parts = lax.all_to_all(
        parts.reshape(devices, rows // devices, -1), "dp", split_axis=0, concat_axis=0, tiled=True
    )
    sums = jnp.sum(parts.astype(F32), axis=0).astype(BF16)
    if tensor == 2:
        sums = sums.astype(F32) + lax.ppermute(sums, "tensor", [(0, 1), (1, 0)]).astype(F32)
    else:
        sums = lax.psum(sums, "tensor").astype(F32)
    ready = jnp.concatenate([normalize(sums[:, :ranks]), sums[:, ranks:].astype(BF16)], axis=1)
    ready = lax.all_gather(ready, "dp", axis=0, tiled=True)
    rank_normed, state_sum = ready[:, :ranks], ready[:, ranks:].astype(F32)

    step_size = jax.nn.softplus(
        jnp.dot(rank_normed, step_local, preferred_element_type=F32)
        + channels(step_bias, me, 0)[None, :]
    )
    lanes = min(128, width)
    in_map = jnp.broadcast_to(state_sum[:, :NS, None], (rows, NS, lanes))
    out_map = jnp.broadcast_to(state_sum[:, NS:, None], (rows, NS, lanes))
    decay = channels(decay_rate, me, 1) * (-1.0 / np.log(2.0)).astype(np.float32)
    restored = channels(state_cache, me, 2) * slot_resume[:, None, None].astype(F32)
    skip = channels(skip_gain, me, 0)[None, :]
    opens = (position == 0).astype(jnp.int32)

    state = jnp.zeros((NS, width), F32)
    partials = []
    for part, cut in enumerate(cuts):
        held, state = scan_rows(
            row_slot[cut], opens[cut], step_size[cut], activated[cut], gate_rows[cut], in_map[cut],
            out_map[cut], decay, restored, skip, state,
        )
        total = jnp.zeros((part_rows, out_weight.shape[1]), F32)
        for step in range(chips):
            mine, other = block_at(core, step), block_at(1 - core, step)
            theirs = lax.ppermute(held, "dp", across)
            total = total + jnp.dot(
                held, channels(out_weight, mine, 0), preferred_element_type=F32
            )
            total = total + jnp.dot(
                theirs, channels(out_weight, other, 0), preferred_element_type=F32
            )
            if step < chips - 1:
                held = lax.ppermute(held, "dp", along)
        partials.append(total.astype(BF16))
    if tensor == 2:
        first = lax.axis_index("tensor") == 0
        send = jnp.where(first, partials[1], partials[0])
        keep = jnp.where(first, partials[0], partials[1])
        got = lax.ppermute(send, "tensor", [(0, 1), (1, 0)])
        return (keep.astype(F32) + got.astype(F32)).astype(BF16)
    return lax.psum_scatter(
        jnp.concatenate(partials, axis=0), "tensor", scatter_dimension=0, tiled=True
    )


def solution(mesh):
    return jax.shard_map(
        shards,
        mesh=mesh,
        in_specs=(
            P("dp", None),
            P(),
            P(),
            P(),
            P(None, "dp", "tensor"),
            P(None, "tensor"),
            P("tensor"),
            P("tensor", None),
            P("tensor", None),
            P("dp", "tensor"),
            P("tensor"),
            P(None, "tensor"),
            P("tensor"),
            P(None, None, "tensor"),
            P(None, None, "tensor"),
            P("tensor", "dp"),
        ),
        out_specs=P("tensor", "dp"),
        check_vma=False,
    )
```

```python
import jax
import jax.numpy as jnp
import numpy as np
from jax import lax
from jax.experimental import pallas as pl
from jax.experimental.pallas import tpu as pltpu
from jax.sharding import PartitionSpec as P

NS = 16
CONV = 4
F32 = jnp.float32
BF16 = jnp.bfloat16


def rings(devices):
    chips = devices // 2
    order = list(range(0, chips, 2)) + list(range(0, chips, 2))[::-1]
    order = [c if i < (chips + 1) // 2 else c + 1 for i, c in enumerate(order)][:chips]
    table = np.array([order, [order[-p % chips] for p in range(chips)]], np.int32)
    place = np.zeros((2, chips), np.int32)
    for core in range(2):
        place[core, table[core]] = np.arange(chips)
    along = [
        (2 * int(table[core, p]) + core, 2 * int(table[core, (p + 1) % chips]) + core)
        for core in range(2)
        for p in range(chips)
    ]
    across = [(i, i ^ 1) for i in range(devices)]
    return chips, table, place, along, across


def normalize(rank_sum):
    return (
        rank_sum * lax.rsqrt(jnp.mean(rank_sum * rank_sum, axis=1, keepdims=True) + 1e-06)
    ).astype(BF16)


def scan_kernel(
    slot_ref, open_ref, step_ref, act_ref, gate_ref, in_ref, out_map_ref, decay_ref, restored_ref,
    skip_ref, init_ref, gated_ref, last_ref, state_ref, drive_ref, sums_ref,
):
    block = pl.program_id(0)
    rows, width = step_ref.shape
    copies = width // in_ref.shape[2]

    @pl.when(block == 0)
    def _():
        state_ref[...] = init_ref[...]

    drive_ref[...] = step_ref[...] * act_ref[...].astype(F32)
    decay = decay_ref[...]

    def wide(a):
        return a if copies == 1 else jnp.concatenate([a] * copies, axis=1)

    def group(g, state):
        for r in range(8):
            t = g * 8 + r
            row = block * rows + t
            opening = jnp.full(state.shape, open_ref[row], jnp.int32) > 0
            prior = jnp.where(opening, restored_ref[slot_ref[row]], state)
            fading = jnp.exp2(step_ref[pl.ds(t, 1), :] * decay)
            state = fading * prior + drive_ref[pl.ds(t, 1), :] * wide(in_ref[t])
            sums_ref[pl.ds(t, 1), :] = jnp.sum(wide(out_map_ref[t]) * state, axis=0, keepdims=True)
        return state

    state = lax.fori_loop(0, rows // 8, group, state_ref[...])
    state_ref[...] = state
    last_ref[...] = state
    gate = gate_ref[...].astype(F32)
    scan_out = sums_ref[...] + skip_ref[...] * act_ref[...].astype(F32)
    gated_ref[...] = (scan_out * (gate / (1.0 + jnp.exp(-gate)))).astype(BF16)


def scan_rows(slots, opens, step, act, gate, in_map, out_map, decay, restored, skip, init):
    total, width = step.shape
    rows = 128
    lanes = in_map.shape[2]
    by_row = pl.BlockSpec((rows, width), lambda i, *_: (i, 0))
    maps = pl.BlockSpec((rows, NS, lanes), lambda i, *_: (i, 0, 0))

    def whole(a):
        return pl.BlockSpec(a.shape, lambda i, *_: (0,) * a.ndim)

    return pl.pallas_call(
        scan_kernel,
        out_shape=(
            jax.ShapeDtypeStruct((total, width), BF16),
            jax.ShapeDtypeStruct((NS, width), F32),
        ),
        grid_spec=pltpu.PrefetchScalarGridSpec(
            num_scalar_prefetch=2,
            grid=(total // rows,),
            in_specs=[by_row, by_row, by_row, maps, maps]
            + [whole(a) for a in (decay, restored, skip, init)],
            out_specs=(by_row, whole(init)),
            scratch_shapes=[
                pltpu.VMEM((NS, width), F32),
                pltpu.VMEM((rows, width), F32),
                pltpu.VMEM((rows, width), F32),
            ],
        ),
        compiler_params=pltpu.CompilerParams(vmem_limit_bytes=32 * 1024 * 1024),
        cost_estimate=pl.CostEstimate(
            flops=total * NS * width * 8,
            bytes_accessed=total * (2 * NS * lanes * 4 + width * 10),
            transcendentals=total * NS * width,
        ),
    )(slots, opens, step, act, gate, in_map, out_map, decay, restored, skip, init)


def shards(
    tokens,
    span_lengths,
    resume,
    slot_ids,
    in_weight,
    conv_weight,
    conv_bias,
    rank_weight,
    state_weight,
    step_weight,
    step_bias,
    decay_rate,
    skip_gain,
    conv_cache,
    state_cache,
    out_weight,
):
    devices = lax.axis_size("dp")
    tensor = lax.axis_size("tensor")
    rows = tokens.shape[0] * devices
    width = in_weight.shape[2] // devices
    ranks = rank_weight.shape[1]
    spans = span_lengths.shape[0]
    me = lax.axis_index("dp")
    core, chip = me % 2, me // 2
    chips, table, place, along, across = rings(devices)
    table, place = jnp.asarray(table), jnp.asarray(place)

    def channels(a, owner, axis):
        return lax.dynamic_slice_in_dim(a, owner * width, width, axis)

    def block_at(which, step):
        return 2 * table[which, (place[which, chip] - step) % chips] + which

    columns = lax.all_to_all(tokens, "dp", split_axis=1, concat_axis=0, tiled=True)

    part_rows = rows // 2
    cuts = [slice(part * part_rows, (part + 1) * part_rows) for part in range(2)]

    halves = []
    for half in range(2):
        arrived = None
        for step in range(chips):
            mine, other = block_at(core, step + 1), block_at(1 - core, step + 1)
            theirs = jnp.dot(
                columns, channels(in_weight[half], other, 1), preferred_element_type=F32
            ).astype(BF16)
            own = jnp.dot(
                columns, channels(in_weight[half], mine, 1), preferred_element_type=F32
            ).astype(BF16)
            total = own.astype(F32) + lax.ppermute(theirs, "dp", across).astype(F32)
            if step > 0:
                total = total + arrived.astype(F32)
            total = total.astype(BF16)
            if step < chips - 1:
                arrived = lax.ppermute(total, "dp", along)
                if half == 0 and step == 1:
                    arrived, step_weight = lax.optimization_barrier((arrived, step_weight))
                    step_local = lax.all_to_all(
                        step_weight, "dp", split_axis=1, concat_axis=0, tiled=True
                    )
                if half == 0 and step == chips // 2:
                    arrived, step_local = lax.optimization_barrier((arrived, step_local))
        halves.append(total)
    inner_rows, gate_rows = halves

    span_ends = jnp.cumsum(span_lengths)
    span_starts = span_ends - span_lengths
    row_ids = jnp.arange(rows, dtype=jnp.int32)
    owners = jnp.sum((span_ends[None, :] <= row_ids[:, None]).astype(jnp.int32), axis=1)
    one_hot = (owners[:, None] == jnp.arange(spans, dtype=jnp.int32)[None, :]).astype(jnp.int32)
    position = row_ids - jnp.sum(one_hot * span_starts[None, :], axis=1)
    row_slot = jnp.sum(one_hot * slot_ids[None, :], axis=1)
    row_resume = jnp.sum(one_hot * resume[None, :], axis=1)
    slots = jnp.arange(spans, dtype=jnp.int32)
    slot_resume = jnp.sum((slot_ids[:, None] == slots[None, :]) * resume[:, None], axis=0)

    slot_cache = channels(conv_cache, me, 2).reshape(spans * (CONV - 1), width)
    inner_wide = inner_rows.astype(F32)
    taps = channels(conv_weight, me, 1)
    convolved = channels(conv_bias, me, 0)[None, :] + taps[0][None, :] * inner_wide
    for lagged in range(1, CONV):
        earlier = jnp.concatenate(
            [jnp.zeros((lagged, width), F32), inner_wide[: rows - lagged]], axis=0
        )
        wanted = jnp.where(
            (position < lagged) & (row_resume > 0),
            row_slot * (CONV - 1) + CONV - 1 + position - lagged,
            -1,
        )
        pick = (
            wanted[:, None] == jnp.arange(spans * (CONV - 1), dtype=jnp.int32)[None, :]
        ).astype(BF16)
        from_cache = jnp.dot(pick, slot_cache, preferred_element_type=F32)
        convolved = convolved + taps[lagged][None, :] * jnp.where(
            (position >= lagged)[:, None], earlier, from_cache
        )
    activated = jax.nn.silu(convolved).astype(BF16)

    both = jnp.concatenate([channels(rank_weight, me, 0), channels(state_weight, me, 0)], axis=1)
    parts = jnp.dot(activated, both, preferred_element_type=F32).astype(BF16)
    parts = lax.all_to_all(
        parts.reshape(devices, rows // devices, -1), "dp", split_axis=0, concat_axis=0, tiled=True
    )
    sums = jnp.sum(parts.astype(F32), axis=0).astype(BF16)
    if tensor == 2:
        sums = sums.astype(F32) + lax.ppermute(sums, "tensor", [(0, 1), (1, 0)]).astype(F32)
    else:
        sums = lax.psum(sums, "tensor").astype(F32)
    ready = jnp.concatenate([normalize(sums[:, :ranks]), sums[:, ranks:].astype(BF16)], axis=1)
    ready = lax.all_gather(ready, "dp", axis=0, tiled=True)
    rank_normed, state_sum = ready[:, :ranks], ready[:, ranks:].astype(F32)

    step_size = jax.nn.softplus(
        jnp.dot(rank_normed, step_local, preferred_element_type=F32)
        + channels(step_bias, me, 0)[None, :]
    )
    lanes = min(128, width)
    in_map = jnp.broadcast_to(state_sum[:, :NS, None], (rows, NS, lanes))
    out_map = jnp.broadcast_to(state_sum[:, NS:, None], (rows, NS, lanes))
    decay = channels(decay_rate, me, 1) * (-1.0 / np.log(2.0)).astype(np.float32)
    restored = channels(state_cache, me, 2) * slot_resume[:, None, None].astype(F32)
    skip = channels(skip_gain, me, 0)[None, :]
    opens = (position == 0).astype(jnp.int32)

    state = jnp.zeros((NS, width), F32)
    partials = []
    for part, cut in enumerate(cuts):
        held, state = scan_rows(
            row_slot[cut], opens[cut], step_size[cut], activated[cut], gate_rows[cut], in_map[cut],
            out_map[cut], decay, restored, skip, state,
        )
        total = jnp.zeros((part_rows, out_weight.shape[1]), F32)
        for step in range(chips):
            mine, other = block_at(core, step), block_at(1 - core, step)
            theirs = lax.ppermute(held, "dp", across)
            total = total + jnp.dot(
                held, channels(out_weight, mine, 0), preferred_element_type=F32
            )
            total = total + jnp.dot(
                theirs, channels(out_weight, other, 0), preferred_element_type=F32
            )
            if step < chips - 1:
                held = lax.ppermute(held, "dp", along)
        partials.append(total.astype(BF16))
    if tensor == 2:
        first = lax.axis_index("tensor") == 0
        send = jnp.where(first, partials[1], partials[0])
        keep = jnp.where(first, partials[0], partials[1])
        got = lax.ppermute(send, "tensor", [(0, 1), (1, 0)])
        return (keep.astype(F32) + got.astype(F32)).astype(BF16)
    return lax.psum_scatter(
        jnp.concatenate(partials, axis=0), "tensor", scatter_dimension=0, tiled=True
    )


def solution(mesh):
    return jax.shard_map(
        shards,
        mesh=mesh,
        in_specs=(
            P("dp", None),
            P(),
            P(),
            P(),
            P(None, "dp", "tensor"),
            P(None, "tensor"),
            P("tensor"),
            P("tensor", None),
            P("tensor", None),
            P("dp", "tensor"),
            P("tensor"),
            P(None, "tensor"),
            P("tensor"),
            P(None, None, "tensor"),
            P(None, None, "tensor"),
            P("tensor", "dp"),
        ),
        out_specs=P("tensor", "dp"),
        check_vma=False,
    )
```
